1024 devices in a mesh: group: 16 (over y_hi, z), expert: 16 (over x, core), tp: 4 (over y_lo).
Axes of the slice: x: 8, y: 8 (y_hi: 2, y_lo: 4; y = y_hi * 4 + y_lo), z: 8, core: 2. Of those that a mesh axis runs over, the one named last changes fastest.
Arguments:
- grad_out: bfloat16 [4096, 3584], P(('group', 'expert'), 'tp'), may hold values from -2 to 2
- route_weights: bfloat16 [4096, 8], P(('group', 'expert')), may hold values from 0.19921875 to 2.5
- expert_ids: int32 [4096, 8], P(('group', 'expert')), may hold values from 0 to 127, as said below
- w_gate: bfloat16 [256, 3584, 512], P(('group', 'expert'), None, 'tp'), may hold values from -0.09375 to 0.09375
- w_up: bfloat16 [256, 3584, 512], P(('group', 'expert'), None, 'tp'), may hold values from -0.09375 to 0.09375
- w_down: bfloat16 [256, 512, 3584], P(('group', 'expert'), 'tp'), may hold values from -0.09375 to 0.09375
- saved_gate: bfloat16 [131072, 512], P(('group', 'expert'), 'tp'), may hold values from -5 to 5
- saved_up: bfloat16 [131072, 512], P(('group', 'expert'), 'tp'), may hold values from -5 to 5
Outputs:
- grad_in: float32 [4096, 3584], P(('group', 'expert'), 'tp')
- grad_route: float32 [4096, 8], P(('group', 'expert'))
The draws below stay inside these ranges and needn't reach their ends.
Inputs may be any that keep to these rules, and one draw needn't show every extreme that they name: `expert_ids`: each row names 8 different experts, two in each of 4 of the 8 node groups (expert e lies in node group e // 16); among the 16 tokens of one device no expert is named more than 2 times, and some device reaches 2.
All inputs are finite; a program needn't handle non-finite values.
Results may differ from the reference program's by a relative error of at most 0.014.
Values may be sent and summed in bfloat16 or wider, within the bound.
A program may use at most 32 MiB of HBM per device.

```python
import math
import jax
import jax.numpy as jnp
from jax import lax

D = 3584
HID = 1024
TOK_DEV = 16
TOKENS = 4096
NODE_GROUPS = 8
LIMIT = 4
TOPK = 8
EXPERTS = 128
EPN = 16
MOST = 2
POSITIONS = 256
SLOTS = 512
HBLK = 128
N_TP = 4


def draw_expert_ids(key, part):
    key = jax.random.fold_in(key, 11)
    node_key, order_key, heat_key = jax.random.split(key, 3)
    block_total = TOKENS // TOK_DEV
    row_keys = jax.random.split(node_key, TOKENS)
    shuffled = jax.vmap(lambda row_key: jax.random.permutation(row_key, NODE_GROUPS))(row_keys)
    chosen = jnp.sort(shuffled[:, :LIMIT], axis=1).astype(jnp.int32)
    member = jnp.sum((chosen[:, :, None] == jnp.arange(NODE_GROUPS, dtype=jnp.int32)[None, None, :]).astype(jnp.int32), axis=1)
    member = member.reshape(block_total, TOK_DEV, NODE_GROUPS)
    before = (jnp.cumsum(member, axis=1) - member).reshape(TOKENS, NODE_GROUPS)
    rank_in = jnp.take_along_axis(before, chosen, axis=1)
    hotness = jax.random.randint(heat_key, (NODE_GROUPS, EPN), 0, 4)
    jitter = jax.random.randint(order_key, (block_total, NODE_GROUPS, EPN), 0, 4)
    scores = (jitter - 2 * hotness[None, :, :]) * EPN + jnp.arange(EPN, dtype=jnp.int32)[None, None, :]
    orders = jnp.argsort(scores, axis=2).astype(jnp.int32)
    block_of = jnp.arange(TOKENS, dtype=jnp.int32) // TOK_DEV
    token_orders = orders[block_of[:, None], chosen]
    spots = (2 * rank_in[:, :, None] + jnp.arange(2, dtype=jnp.int32)[None, None, :]) % EPN
    within = jnp.take_along_axis(token_orders, spots, axis=2)
    return (chosen[:, :, None] * EPN + within).reshape(TOKENS, TOPK).astype(jnp.int32)


def block_scale(key, extent, shards, least, top_value):
    factor_of = 1.0
    for position, shards_of in shards:
        draws = jax.random.uniform(jax.random.fold_in(jax.random.fold_in(key, 6), position), (shards_of,), jnp.float32, least / len(shards), top_value / len(shards))
        factor_of = factor_of * jnp.repeat(jnp.exp(draws), extent[position] // shards_of).reshape((-1,) + (1,) * (len(extent) - 1 - position))
    return factor_of


def centred(rng, extent, spread, bound, cuts=(), kind=jnp.bfloat16):
    level = block_scale(rng, extent, cuts, -0.22, 0.18) if cuts else 1.0
    values = jax.random.normal(rng, extent, jnp.float32) * spread * level
    return jnp.minimum(jnp.maximum(values, -bound), bound).astype(kind)


def setup_inputs(seed: int = 0) -> dict:
    key_list = jax.random.split(jax.random.key(seed), 9)
    return {
        "grad_out": centred(key_list[0], (TOKENS, D), 0.3, 2.0, ((0, 256), (1, 4))),
        "route_weights": jnp.clip(jnp.exp(math.log(2.5) - 2.5296425 * jax.random.uniform(key_list[1], (TOKENS, TOPK), jnp.float32) ** block_scale(key_list[1], (TOKENS, TOPK), ((0, 256),), -0.2, 0.2)), 0.19921875, 2.5).astype(jnp.bfloat16),
        "expert_ids": draw_expert_ids(jax.random.fold_in(key_list[8], 71), 0),
        "w_gate": centred(key_list[3], (POSITIONS, D, HID // 2), D ** -0.5, 0.09375, ((0, 256), (2, 4))),
        "w_up": centred(key_list[4], (POSITIONS, D, HID // 2), D ** -0.5, 0.09375, ((0, 256), (2, 4))),
        "w_down": centred(key_list[5], (POSITIONS, HID // 2, D), D ** -0.5, 0.09375, ((0, 256), (1, 4))),
        "saved_gate": centred(key_list[6], (POSITIONS * SLOTS, HID // 2), 1.0, 5.0, ((0, 256), (1, 4))),
        "saved_up": centred(key_list[7], (POSITIONS * SLOTS, HID // 2), 1.0, 5.0, ((0, 256), (1, 4))),
    }


def block_ranks(expert_ids):
    block_total = TOKENS // TOK_DEV
    pair_count = TOK_DEV * TOPK
    flat_ids = expert_ids.reshape(block_total, pair_count)
    owner_token = jnp.arange(pair_count, dtype=jnp.int32) // TOPK
    earlier = owner_token[None, :] < owner_token[:, None]
    same_expert = flat_ids[:, :, None] == flat_ids[:, None, :]
    rank_of = jnp.sum(jnp.logical_and(same_expert, earlier[None, :, :]).astype(jnp.int32), axis=2).astype(jnp.int32)
    return flat_ids, rank_of


def join_halves(array, expert_index):
    return lax.dynamic_slice_in_dim(array, (2 * expert_index).astype(jnp.int32), 2, 0)


def reference(grad_out, route_weights, expert_ids, w_gate, w_up, w_down, saved_gate, saved_up):
    block_total = TOKENS // TOK_DEV
    pair_count = TOK_DEV * TOPK
    half_width = HID // 2
    block_count = 2 * N_TP
    flat_ids, rank_of = block_ranks(expert_ids)
    weights_flat = route_weights.reshape(block_total, pair_count).astype(jnp.float32)
    source = grad_out.reshape(block_total, TOK_DEV, D).astype(jnp.float32)
    level_ids = jnp.arange(MOST, dtype=jnp.int32)
    levels_hit = (rank_of[:, :, None] == level_ids[None, None, :]).astype(jnp.float32)
    gate_saved = saved_gate.reshape(POSITIONS, SLOTS, half_width)
    up_saved = saved_up.reshape(POSITIONS, SLOTS, half_width)
    highest = lax.Precision.HIGHEST

    def one_expert(carry, expert_index):
        grad_sum, route_total = carry
        matched = (flat_ids == expert_index).astype(jnp.float32)
        choose = (matched[:, :, None] * levels_hit).reshape(block_total, TOK_DEV, TOPK, MOST).sum(axis=2)
        routed_rows = jnp.einsum("bim,bid->bmd", choose, source, precision=highest)
        routed_rows = routed_rows.reshape(SLOTS, D).astype(jnp.bfloat16)
        gate_w = join_halves(w_gate, expert_index).transpose(1, 0, 2).reshape(D, HID)
        up_w = join_halves(w_up, expert_index).transpose(1, 0, 2).reshape(D, HID)
        down_w = join_halves(w_down, expert_index).reshape(HID, D)
        gate_pre = join_halves(gate_saved, expert_index).transpose(1, 0, 2).reshape(SLOTS, HID).astype(jnp.float32)
        up_pre = join_halves(up_saved, expert_index).transpose(1, 0, 2).reshape(SLOTS, HID).astype(jnp.float32)
        adjoint = jnp.dot(routed_rows, down_w.T, preferred_element_type=jnp.float32)
        gate_sigmoid = jax.nn.sigmoid(gate_pre)
        activated = gate_pre * gate_sigmoid
        slot_route = jnp.sum(activated * up_pre * adjoint, axis=1)
        d_gate = (adjoint * up_pre * gate_sigmoid * (1.0 + gate_pre * (1.0 - gate_sigmoid))).astype(jnp.bfloat16)
        d_up = (adjoint * activated).astype(jnp.bfloat16)
        block_terms = jnp.einsum("sch,dch->csd", d_gate.reshape(SLOTS, block_count, HBLK).astype(jnp.float32),
                                 gate_w.reshape(D, block_count, HBLK).astype(jnp.float32), precision=highest)
        block_terms = block_terms + jnp.einsum("sch,dch->csd", d_up.reshape(SLOTS, block_count, HBLK).astype(jnp.float32),
                                               up_w.reshape(D, block_count, HBLK).astype(jnp.float32), precision=highest)
        block_terms = lax.optimization_barrier(block_terms.astype(jnp.bfloat16))
        returned = jnp.sum(block_terms.astype(jnp.float32), axis=0)
        weighted = ((matched * weights_flat)[:, :, None] * levels_hit).reshape(block_total, TOK_DEV, TOPK, MOST).sum(axis=2)
        grad_sum = grad_sum + jnp.einsum("bim,bmd->bid", weighted, returned.reshape(block_total, MOST, D), precision=highest)
        picked = jnp.take_along_axis(slot_route.reshape(block_total, MOST), rank_of, axis=1)
        route_total = route_total + matched * picked
        return (grad_sum, route_total), None

    start_carry = (jnp.zeros((block_total, TOK_DEV, D), jnp.float32), jnp.zeros((block_total, pair_count), jnp.float32))
    (grad_sum, route_total), _ = lax.scan(one_expert, start_carry, jnp.arange(EXPERTS, dtype=jnp.int32))
    return grad_sum.reshape(TOKENS, D), route_total.reshape(TOKENS, TOPK)
```

```python
import functools

import jax
import jax.numpy as jnp
from jax import lax
from jax.experimental import pallas as pl
from jax.experimental.pallas import tpu as pltpu
from jax.sharding import PartitionSpec as P

MESH = pl.DeviceIdType.MESH
F32 = jnp.float32
BF16 = jnp.bfloat16
TP = 4
TOK = 16
META = 128


def dot_nn(left, right):
    return lax.dot_general(left, right, (((1,), (0,)), ((), ())), preferred_element_type=F32)


def dot_nt(left, right):
    return lax.dot_general(left, right, (((1,), (1,)), ((), ())), preferred_element_type=F32)


def rcopy(src, dst, send, recv, device):
    return pltpu.make_async_remote_copy(
        src_ref=src, dst_ref=dst, send_sem=send, recv_sem=recv, device_id=device, device_id_type=MESH
    )


def step_of(j, count):
    odd = j % 2
    return odd * ((j + 1) // 2) + (1 - odd) * ((count - j // 2) % count)


def kernel(
    nx, nz, width,
    tok, wg_hbm, wu_hbm, wd_hbm, sg_hbm, su_hbm,
    gin_ref, grt_ref,
    T, SEL, SMAT, SWT, IDW, RH, WD, WG, WU, SG, SU, A1, A2, A3, TM, RT, RTS, RTR, ZTS, ZTR,
    SR, SL, RR, RL, ZS, ZRET, OUT, XR, HS, HB, HR,
    lsem, ws, wr, hs, hr, xs, xr, zs, zr, ags, agr, rss, rsr, zbs, zbr, rts, rtr, zts, ztr, xbs, xbr,
):
    g = lax.axis_index("group")
    e = lax.axis_index("expert")
    q = lax.axis_index("tp")
    h, z = g // nz, g % nz
    x, c = e // 2, e % 2
    nb = 2 * nx
    ntok = nb * TOK
    sp = 2 * nb
    nslot = nz * sp
    hid = 128

    def dev_x(k):
        return {"expert": ((x + k) % nx) * 2 + c}

    def dev_z(zz):
        return {"group": h * nz + zz}

    sibling = {"expert": x * 2 + (1 - c)}
    partner = {"group": (1 - h) * nz + z}

    pairs = (
        (sg_hbm, SG.at[0], SG.at[1]),
        (su_hbm, SU.at[0], SU.at[1]),
        (wd_hbm.at[0], WD.at[pl.ds(0, hid), :], WD.at[pl.ds(hid, hid), :]),
        (wg_hbm.at[0], WG.at[:, pl.ds(0, hid)], WG.at[:, pl.ds(hid, hid)]),
        (wu_hbm.at[0], WU.at[:, pl.ds(0, hid)], WU.at[:, pl.ds(hid, hid)]),
    )
    local = [pltpu.make_async_copy(src, own, lsem.at[i]) for i, (src, own, _) in enumerate(pairs)]
    for copy in local:
        copy.start()

    barrier = pltpu.get_barrier_semaphore()
    for k in range(1, nx):
        pl.semaphore_signal(barrier, inc=1, device_id=dev_x(k), device_id_type=MESH)
    for k in range(1, nz):
        pl.semaphore_signal(barrier, inc=1, device_id=dev_z((z + k) % nz), device_id_type=MESH)
    for k in range(1, TP):
        pl.semaphore_signal(barrier, inc=1, device_id={"tp": (q + k) % TP}, device_id_type=MESH)
    pl.semaphore_signal(barrier, inc=1, device_id=sibling, device_id_type=MESH)
    pl.semaphore_signal(barrier, inc=1, device_id=partner, device_id_type=MESH)
    pl.semaphore_wait(barrier, nx + nz + TP - 1)

    to_partner = rcopy(tok, T.at[x, h], hs.at[0], hr.at[0], partner)
    to_partner.start()
    own_x = [rcopy(tok, T.at[x, h], xs.at[0, k], xr.at[h, x], dev_x(k)) for k in range(1, nx)]
    for copy in own_x:
        copy.start()
    T[x, h] = tok[...]
    siblings = [rcopy(src, far, ws.at[i], wr.at[i], sibling) for i, (src, _, far) in enumerate(pairs)]
    for copy in siblings:
        copy.start()
    rcopy(tok, T.at[x, 1 - h], hs.at[0], hr.at[0], partner).wait_recv()
    far_x = [
        rcopy(T.at[x, 1 - h], T.at[x, 1 - h], xs.at[1, k], xr.at[1 - h, x], dev_x(k)) for k in range(1, nx)
    ]
    for copy in far_x:
        copy.start()

    for i in range(2):
        local[i].wait()
        siblings[i].wait_recv()
    row = lax.broadcasted_iota(jnp.int32, (nslot, 8 * nx * nz), 0)
    col = lax.broadcasted_iota(jnp.int32, (nslot, 8 * nx * nz), 1)
    j_of, rest = row // sp, row % sp
    z_of = (z + step_of(j_of, nz)) % nz
    where_of = ((((rest // 2) % 2) * nz + z_of) * nx + rest // 4) * 4 + c * 2 + rest % 2
    pick = (where_of == col).astype(F32).astype(BF16)
    for s in range(2):
        gate = dot_nn(pick, SG[s])
        up = dot_nn(pick, SU[s])
        sigma = jax.nn.sigmoid(gate)
        act = gate * sigma
        lanes = pl.ds(s * hid, hid)
        A1[:, :, lanes] = (up * sigma * (1.0 + gate * (1.0 - sigma))).reshape(nz, sp, hid)
        A2[:, :, lanes] = act.reshape(nz, sp, hid)
        A3[:, :, lanes] = (act * up).reshape(nz, sp, hid)

    for hb in range(2):
        for k in range(1, nx):
            src_x = (x + k) % nx
            rcopy(T.at[src_x, hb], T.at[src_x, hb], xs.at[0, k], xr.at[hb, src_x], dev_x(k)).wait_recv()

    meta = T[:, :, :, pl.ds(width, META)].reshape(ntok, META).astype(F32)
    meta_t = jnp.transpose(meta)
    IDW[...] = meta_t[0:16, :]
    ids8 = IDW[0:8, :]
    w8 = IDW[8:16, :]

    def expert_at(j):
        zz = (z + nz - step_of(j, nz)) % nz
        return ((h * nz + zz) * nx + x).astype(F32)

    match_rows, weight_rows = [], []
    for j in range(nz):
        hit = (ids8 == expert_at(j)).astype(F32)
        match_rows.append(jnp.sum(hit, axis=0, keepdims=True))
        weight_rows.append(jnp.sum(hit * w8, axis=0, keepdims=True))
    t_row = lax.broadcasted_iota(jnp.int32, (ntok, ntok), 0)
    t_col = lax.broadcasted_iota(jnp.int32, (ntok, ntok), 1)
    before = jnp.logical_and(t_row // TOK == t_col // TOK, t_row < t_col).astype(F32).astype(BF16)
    matches = jnp.concatenate(match_rows, axis=0)
    ranks = dot_nn(matches.astype(BF16), before)
    s_row = lax.broadcasted_iota(jnp.int32, (sp, ntok), 0)
    s_block = (s_row // 2 == lax.broadcasted_iota(jnp.int32, (sp, ntok), 1) // TOK).astype(F32)
    s_level = (s_row % 2).astype(F32)
    for j in range(nz):
        chosen = s_block * matches[j:j + 1, :] * (s_level == ranks[j:j + 1, :]).astype(F32)
        SMAT[j] = chosen
    tokens = T[:, :, :, pl.ds(0, width)].reshape(ntok, width)
    selected = dot_nn(SMAT[...].reshape(nslot, ntok).astype(BF16), tokens).astype(BF16)
    SEL[...] = selected.reshape(nz, sp, width)
    for j in range(1, nz):
        zz = (z + nz - step_of(j, nz)) % nz
        rcopy(SEL.at[j], RH.at[q, j], zs.at[j], zr.at[j], dev_z(zz)).start()
    RH[q, 0] = SEL[0]
    weighted = jnp.concatenate([SMAT[j] * weight_rows[j] for j in range(nz)], axis=0)
    SWT[...] = jnp.transpose(weighted).astype(BF16)

    for i in range(2, 5):
        local[i].wait()
        siblings[i].wait_recv()

    def spread(origin, j, way):
        return rcopy(
            RH.at[origin, j], RH.at[origin, j], ags.at[way, origin, j], agr.at[origin, j],
            {"tp": (q + 1 - 2 * way) % TP},
        )

    def passed(s, j, way):
        src, dst = ((SR, RR), (SL, RL))[way]
        return rcopy(
            src.at[s, j], dst.at[s, j], rss.at[way, s, j], rsr.at[way, s, j], {"tp": (q + 1 - 2 * way) % TP}
        )

    def back(j):
        return rcopy(ZS.at[j], ZRET.at[j], zbs.at[j], zbr.at[j], dev_z((z + step_of(j, nz)) % nz))

    def route_tp(k):
        return rcopy(RTS, RTR.at[k - 1], rts.at[k - 1], rtr.at[k - 1], {"tp": (q + k) % TP})

    def route_z(j):
        return rcopy(ZTS, ZTR.at[j], zts.at[j], ztr.at[j], dev_z((z + step_of(j, nz)) % nz))

    def body(t, carry):
        @pl.when(t < nz)
        def _():
            @pl.when(t > 0)
            def _():
                rcopy(SEL.at[t], RH.at[q, t], zs.at[t], zr.at[t], dev_z(z)).wait_recv()

            @pl.when(q < TP - 1)
            def _():
                spread(q, t, 0).start()

            @pl.when(q > 0)
            def _():
                spread(q, t, 1).start()

        for k in range(1, TP):
            j = t - k

            @pl.when(jnp.logical_and(j >= 0, j < nz))
            def _():
                @pl.when(q >= k)
                def _():
                    spread(q - k, j, 0).wait_recv()

                    @pl.when(q < TP - 1)
                    def _():
                        spread(q - k, j, 0).start()

                @pl.when(q + k < TP)
                def _():
                    spread(q + k, j, 1).wait_recv()

                    @pl.when(q > 0)
                    def _():
                        spread(q + k, j, 1).start()

        j = t - (TP - 1)

        @pl.when(jnp.logical_and(j >= 0, j < nz))
        def _():
            adjoint = dot_nt(RH[0, j], WD[:, pl.ds(0, width)])
            for s in range(1, TP):
                adjoint += dot_nt(RH[s, j], WD[:, pl.ds(s * width, width)])
            d_gate = (adjoint * A1[j]).astype(BF16)
            d_up = (adjoint * A2[j]).astype(BF16)
            RT[j] = jnp.broadcast_to(jnp.sum(adjoint * A3[j], axis=1, keepdims=True), (sp, META))
            for s in range(TP):
                part = pl.ds(s * width, width)
                TM[s, j] = dot_nt(d_gate, WG[part, :]) + dot_nt(d_up, WU[part, :])

        @pl.when(t == nz + TP - 2)
        def _():
            RTS[...] = jnp.transpose(RT[...].reshape(nslot, META))[0:8, :]
            for k in range(1, TP):
                route_tp(k).start()

        @pl.when(t == nz + TP - 1)
        def _():
            for k in range(1, TP):
                route_tp(k).wait_recv()
            ZTS[...] = RTS[...] + RTR[0] + RTR[1] + RTR[2]
            ZTR[0] = ZTS[...]
            for i in range(1, nz):
                route_z(i).start()

        for k in range(TP - 1):
            j = t - (TP - 1) - k

            @pl.when(jnp.logical_and(j >= 0, j < nz))
            def _():
                for way in range(2):
                    place = k if way == 0 else TP - 1 - k
                    src, dst = ((SR, RR), (SL, RL))[way]
                    targets = range(TP - 1, k, -1) if way == 0 else range(0, TP - 1 - k)

                    @pl.when(q == place)
                    def _():
                        for s in targets:
                            value = TM[s, j]
                            if k > 0:
                                passed(s, j, way).wait_recv()
                                value = value + dst[s, j].astype(F32)
                            src[s, j] = value.astype(BF16)
                            passed(s, j, way).start()

        j = t - 2 * (TP - 1)

        @pl.when(jnp.logical_and(j >= 0, j < nz))
        def _():
            @pl.when(q > 0)
            def _():
                passed(q, j, 0).wait_recv()
                TM[q, j] = TM[q, j] + RR[q, j].astype(F32)

            @pl.when(q < TP - 1)
            def _():
                passed(q, j, 1).wait_recv()
                TM[q, j] = TM[q, j] + RL[q, j].astype(F32)

            @pl.when(j == 0)
            def _():
                ZRET[0] = TM[q, j].astype(BF16)

            @pl.when(j > 0)
            def _():
                ZS[j] = TM[q, j].astype(BF16)
                back(j).start()

        return carry

    lax.fori_loop(0, nz + 2 * (TP - 1), body, 0)

    for j in range(1, nz):
        route_z(j).wait_recv()
    columns = jnp.transpose(ZTR[...].reshape(nz * 8, nslot))
    ids_now = IDW[0:8, :]
    route = jnp.zeros((8, ntok), F32)
    for j in range(nz):
        column = columns[j * sp:(j + 1) * sp, 8 * j:8 * j + 1]
        value = jnp.sum(SMAT[j] * column, axis=0, keepdims=True)
        route += (ids_now == expert_at(j)).astype(F32) * value
    route_t = jnp.transpose(jnp.concatenate([route, jnp.zeros((META - 8, ntok), F32)], axis=0))
    OUT[:, :, :, pl.ds(width, META)] = route_t.astype(BF16).reshape(nx, 2, TOK, META)

    for j in range(1, nz):
        back(j).wait_recv()
    combined = dot_nn(SWT[...], ZRET[...].reshape(nslot, width)).astype(BF16)
    OUT[:, :, :, pl.ds(0, width)] = combined.reshape(nx, 2, TOK, width)

    def home(k):
        to = (x + k) % nx
        return rcopy(OUT.at[to], XR.at[k], xbs.at[k], xbr.at[k], dev_x(k))

    for k in range(1, nx):
        home(k).start()
    total = OUT[x].astype(F32)
    for k in range(1, nx):
        home(k).wait_recv()
        total += XR[k].astype(F32)
    HS[...] = total
    HB[...] = HS[1 - h].astype(BF16)
    homeward = rcopy(HB, HR, hs.at[1], hr.at[1], partner)
    homeward.start()
    homeward.wait_recv()
    result = HS[h] + HR[...].astype(F32)
    gin_ref[...] = result[:, 0:width]
    grt_ref[...] = result[:, width:width + 8]

    to_partner.wait_send()
    homeward.wait_send()
    for copy in own_x + far_x + siblings:
        copy.wait_send()
    for k in range(1, TP):
        route_tp(k).wait_send()
    for k in range(1, nx):
        home(k).wait_send()
    for j in range(1, nz):
        rcopy(SEL.at[j], RH.at[q, j], zs.at[j], zr.at[j], dev_z(z)).wait_send()
        back(j).wait_send()
        route_z(j).wait_send()

    def drain(j, carry):
        for origin in range(TP):
            @pl.when(jnp.logical_and(q >= origin, q < TP - 1))
            def _():
                spread(origin, j, 0).wait_send()

            @pl.when(jnp.logical_and(q <= origin, q > 0))
            def _():
                spread(origin, j, 1).wait_send()

            @pl.when(q < origin)
            def _():
                passed(origin, j, 0).wait_send()

            @pl.when(q > origin)
            def _():
                passed(origin, j, 1).wait_send()

        return carry

    lax.fori_loop(0, nz, drain, 0)


def shards(grad_out, route_weights, expert_ids, w_gate, w_up, w_down, saved_gate, saved_up):
    width = grad_out.shape[1]
    nz = lax.axis_size("group") // 2
    nx = lax.axis_size("expert") // 2
    nb = 2 * nx
    ntok, sp = nb * TOK, 2 * nb
    nslot = nz * sp
    features = TP * width
    slots = saved_gate.shape[0]
    topk = expert_ids.shape[1]
    tok = jnp.concatenate(
        [grad_out, expert_ids.astype(BF16), route_weights, jnp.zeros((TOK, META - 2 * topk), BF16)], axis=1
    )
    vmem = pltpu.VMEM
    dma = pltpu.SemaphoreType.DMA
    scratch = [
        vmem((nx, 2, TOK, width + META), BF16),
        vmem((nz, sp, width), BF16),
        vmem((nz, sp, ntok), F32),
        vmem((ntok, nslot), BF16),
        vmem((16, ntok), F32),
        vmem((TP, nz, sp, width), BF16),
        vmem((256, features), BF16),
        vmem((features, 256), BF16),
        vmem((features, 256), BF16),
        vmem((2, slots, 128), BF16),
        vmem((2, slots, 128), BF16),
        vmem((nz, sp, 256), F32),
        vmem((nz, sp, 256), F32),
        vmem((nz, sp, 256), F32),
        vmem((TP, nz, sp, width), F32),
        vmem((nz, sp, META), F32),
        vmem((8, nslot), F32),
        vmem((TP - 1, 8, nslot), F32),
        vmem((8, nslot), F32),
        vmem((nz, 8, nslot), F32),
        vmem((TP, nz, sp, width), BF16),
        vmem((TP, nz, sp, width), BF16),
        vmem((TP, nz, sp, width), BF16),
        vmem((TP, nz, sp, width), BF16),
        vmem((nz, sp, width), BF16),
        vmem((nz, sp, width), BF16),
        vmem((nx, 2, TOK, width + META), BF16),
        vmem((nx, 2, TOK, width + META), BF16),
        vmem((2, TOK, width + META), F32),
        vmem((TOK, width + META), BF16),
        vmem((TOK, width + META), BF16),
        dma((5,)), dma((5,)), dma((5,)),
        dma((2,)), dma((2,)),
        dma((2, nx)), dma((2, nx)),
        dma((nz,)), dma((nz,)),
        dma((2, TP, nz)), dma((TP, nz)),
        dma((2, TP, nz)), dma((2, TP, nz)),
        dma((nz,)), dma((nz,)),
        dma((TP - 1,)), dma((TP - 1,)),
        dma((nz,)), dma((nz,)),
        dma((nx,)), dma((nx,)),
    ]
    whole = pl.BlockSpec(memory_space=pltpu.VMEM)
    far = pl.BlockSpec(memory_space=pl.ANY)
    return pl.pallas_call(
        functools.partial(kernel, nx, nz, width),
        out_shape=(
            jax.ShapeDtypeStruct((TOK, width), F32),
            jax.ShapeDtypeStruct((TOK, topk), F32),
        ),
        in_specs=[whole] + [far] * 5,
        out_specs=(whole, whole),
        scratch_shapes=scratch,
        compiler_params=pltpu.CompilerParams(
            collective_id=0, has_side_effects=True, vmem_limit_bytes=48 * 1024 * 1024
        ),
        name="expert_backward",
    )(tok, w_gate, w_up, w_down, saved_gate, saved_up)


def solution(mesh):
    return jax.shard_map(
        shards,
        mesh=mesh,
        in_specs=(
            P(("group", "expert"), "tp"),
            P(("group", "expert"), None),
            P(("group", "expert"), None),
            P(("group", "expert"), None, "tp"),
            P(("group", "expert"), None, "tp"),
            P(("group", "expert"), "tp", None),
            P(("group", "expert"), "tp"),
            P(("group", "expert"), "tp"),
        ),
        out_specs=(P(("group", "expert"), "tp"), P(("group", "expert"), None)),
        check_vma=False,
    )
```

```python
import functools

import jax
import jax.numpy as jnp
from jax import lax
from jax.experimental import pallas as pl
from jax.experimental.pallas import tpu as pltpu
from jax.sharding import PartitionSpec as P

MESH = pl.DeviceIdType.MESH
F32 = jnp.float32
BF16 = jnp.bfloat16
TP = 4
TOK = 16
META = 128


def dot_nn(left, right):
    return lax.dot_general(left, right, (((1,), (0,)), ((), ())), preferred_element_type=F32)


def dot_nt(left, right):
    return lax.dot_general(left, right, (((1,), (1,)), ((), ())), preferred_element_type=F32)


def dot_tn(left, right):
    return lax.dot_general(left, right, (((0,), (0,)), ((), ())), preferred_element_type=F32)


def rcopy(src, dst, send, recv, device):
    return pltpu.make_async_remote_copy(
        src_ref=src, dst_ref=dst, send_sem=send, recv_sem=recv, device_id=device, device_id_type=MESH
    )


def step_of(j, count):
    odd = j % 2
    return odd * ((j + 1) // 2) + (1 - odd) * ((count - j // 2) % count)


def kernel(
    nx, nz, width,
    go_hbm, ids_hbm, rw_hbm, wg_hbm, wu_hbm, wd_hbm, sg_hbm, su_hbm,
    gin_ref, grt_ref,
    tok, IDS, RW, T, SEL, SMAT, SWT, IDW, RH, WD, WG, WU, SG, SU, A1, A2, A3, TM, RT, RTS, RTR, ZTS, ZTR,
    SR, SL, RR, RL, ZS, ZRET, OUT0, OUT1, XR0, XR1, HB, HR,
    lsem, ws, wr, hs, hr, xs, xr, zs, zr, ags, agr, rss, rsr, zbs, zbr, rts, rtr, zts, ztr, xbs, xbr,
):
    g = lax.axis_index("group")
    e = lax.axis_index("expert")
    q = lax.axis_index("tp")
    h, z = g // nz, g % nz
    x, c = e // 2, e % 2
    ntok = nx * TOK
    sp = 2 * nx
    half_slots = nz * sp
    nslot = 2 * half_slots
    per_half = nz // 2
    hid = 128
    slots = 2 * nslot

    def dev_x(k):
        return {"expert": ((x + k) % nx) * 2 + c}

    def dev_z(zz):
        return {"group": h * nz + zz}

    sibling = {"expert": x * 2 + (1 - c)}
    partner = {"group": (1 - h) * nz + z}

    pairs = (
        (sg_hbm, SG.at[0], SG.at[1]),
        (su_hbm, SU.at[0], SU.at[1]),
        (wd_hbm.at[0], WD.at[pl.ds(0, hid), :], WD.at[pl.ds(hid, hid), :]),
        (wg_hbm.at[0], WG.at[:, pl.ds(0, hid)], WG.at[:, pl.ds(hid, hid)]),
        (wu_hbm.at[0], WU.at[:, pl.ds(0, hid)], WU.at[:, pl.ds(hid, hid)]),
    )
    small = [
        pltpu.make_async_copy(go_hbm, tok.at[:, pl.ds(0, width)], lsem.at[5]),
        pltpu.make_async_copy(ids_hbm, IDS, lsem.at[6]),
        pltpu.make_async_copy(rw_hbm, RW, lsem.at[7]),
    ]
    for copy in small:
        copy.start()
    local = [pltpu.make_async_copy(src, own, lsem.at[i]) for i, (src, own, _) in enumerate(pairs)]
    for copy in local:
        copy.start()

    barrier = pltpu.get_barrier_semaphore()
    for k in range(1, nx):
        pl.semaphore_signal(barrier, inc=1, device_id=dev_x(k), device_id_type=MESH)
    for k in range(1, nz):
        pl.semaphore_signal(barrier, inc=1, device_id=dev_z((z + k) % nz), device_id_type=MESH)
    for k in range(1, TP):
        pl.semaphore_signal(barrier, inc=1, device_id={"tp": (q + k) % TP}, device_id_type=MESH)
    pl.semaphore_signal(barrier, inc=1, device_id=sibling, device_id_type=MESH)
    pl.semaphore_signal(barrier, inc=1, device_id=partner, device_id_type=MESH)
    for copy in small:
        copy.wait()
    lane = lax.broadcasted_iota(jnp.int32, (8, META), 1)
    entry = lax.broadcasted_iota(jnp.int32, (8, META), 0)
    tok[:, pl.ds(width, META)] = (
        dot_tn(IDS[...].astype(F32).astype(BF16), (lane == entry).astype(F32).astype(BF16))
        + dot_tn(RW[...], (lane == entry + 8).astype(F32).astype(BF16))
    ).astype(BF16)
    pl.semaphore_wait(barrier, nx + nz + TP - 1)

    def along_x(half, k):
        src = tok if half == 0 else T.at[1, x]
        return rcopy(src, T.at[half, x], xs.at[half, k], xr.at[half, x], dev_x(k))

    def arrives_x(half, k):
        origin = (x + k) % nx
        return rcopy(tok, T.at[half, origin], xs.at[half, k], xr.at[half, origin], dev_x(k))

    to_partner = rcopy(tok, T.at[1, x], hs.at[0], hr.at[0], partner)
    to_partner.start()
    for k in range(1, nx):
        along_x(0, k).start()
    T[0, x] = tok[...]
    siblings = [rcopy(src, far, ws.at[i], wr.at[i], sibling) for i, (src, _, far) in enumerate(pairs)]
    for copy in siblings:
        copy.start()
    to_partner.wait_recv()
    for k in range(1, nx):
        along_x(1, k).start()

    for i in range(2):
        local[i].wait()
        siblings[i].wait_recv()
    rest = lax.broadcasted_iota(jnp.int32, (sp, slots), 0)
    col = lax.broadcasted_iota(jnp.int32, (sp, slots), 1)
    within = ((rest >> 1) << 2) + (rest & 1) + c * 2
    pieces = []
    for half in (h, 1 - h):
        for j in range(nz):
            first = (half * nz + (z + step_of(j, nz)) % nz) * (4 * nx)
            pieces.append((within == col - first).astype(F32))
    pick = jnp.concatenate(pieces, axis=0).astype(BF16)
    for s in range(2):
        gate = dot_nn(pick, SG[s])
        up = dot_nn(pick, SU[s])
        sigma = jax.nn.sigmoid(gate)
        act = gate * sigma
        lanes = pl.ds(s * hid, hid)
        A1[:, :, lanes] = (up * sigma * (1.0 + gate * (1.0 - sigma))).reshape(nz, 2 * sp, hid)
        A2[:, :, lanes] = act.reshape(nz, 2 * sp, hid)
        A3[:, :, lanes] = (act * up).reshape(nz, 2 * sp, hid)

    def expert_at(j):
        zz = (z + nz - step_of(j, nz)) % nz
        return ((h * nz + zz) * nx + x).astype(F32)

    def slot_rows(half, j):
        return rcopy(
            SEL.at[half, j], RH.at[q, half * per_half + j // 2, j % 2], zs.at[half, j], zr.at[half, j],
            dev_z((z + nz - step_of(j, nz)) % nz),
        )

    def choose(half):
        for k in range(1, nx):
            arrives_x(half, k).wait_recv()
        meta_t = jnp.transpose(T[half, :, :, pl.ds(width, META)].reshape(ntok, META).astype(F32))
        IDW[half] = meta_t[0:16, :]
        ids8 = IDW[half, 0:8, :]
        w8 = IDW[half, 8:16, :]
        match_rows, weight_rows = [], []
        for j in range(nz):
            hit = (ids8 == expert_at(j)).astype(F32)
            match_rows.append(jnp.sum(hit, axis=0, keepdims=True))
            weight_rows.append(jnp.sum(hit * w8, axis=0, keepdims=True))
        t_row = lax.broadcasted_iota(jnp.int32, (ntok, ntok), 0)
        t_col = lax.broadcasted_iota(jnp.int32, (ntok, ntok), 1)
        before = jnp.logical_and(t_row >> 4 == t_col >> 4, t_row < t_col).astype(F32).astype(BF16)
        matches = jnp.concatenate(match_rows, axis=0)
        ranks = dot_nn(matches.astype(BF16), before)
        s_row = lax.broadcasted_iota(jnp.int32, (sp, ntok), 0)
        s_block = (s_row >> 1 == lax.broadcasted_iota(jnp.int32, (sp, ntok), 1) >> 4).astype(F32)
        s_level = (s_row & 1).astype(F32)
        for j in range(nz):
            SMAT[half, j] = s_block * matches[j:j + 1, :] * (s_level == ranks[j:j + 1, :]).astype(F32)
        tokens = T[half, :, :, pl.ds(0, width)].reshape(ntok, width)
        selected = dot_nn(SMAT[half].reshape(half_slots, ntok).astype(BF16), tokens).astype(BF16)
        SEL[half] = selected.reshape(nz, sp, width)
        for j in range(1, nz):
            slot_rows(half, j).start()
        RH[q, half * per_half, 0] = SEL[half, 0]
        weighted = jnp.concatenate([SMAT[half, j] * weight_rows[j] for j in range(nz)], axis=0)
        SWT[half] = jnp.transpose(weighted).astype(BF16)

    choose(0)

    def spread(origin, i, way):
        return rcopy(
            RH.at[origin, i], RH.at[origin, i], ags.at[way, origin, i], agr.at[origin, i],
            {"tp": (q + 1 - 2 * way) % TP},
        )

    def passed(s, i, way):
        src, dst = ((SR, RR), (SL, RL))[way]
        return rcopy(
            src.at[s, i], dst.at[s, i], rss.at[way, s, i], rsr.at[way, s, i], {"tp": (q + 1 - 2 * way) % TP}
        )

    def back(half, j):
        return rcopy(
            ZS.at[half * per_half + j // 2, j % 2], ZRET.at[half, j], zbs.at[half, j], zbr.at[half, j],
            dev_z((z + step_of(j, nz)) % nz),
        )

    def route_tp(k):
        return rcopy(RTS, RTR.at[k - 1], rts.at[k - 1], rtr.at[k - 1], {"tp": (q + k) % TP})

    def route_z(j):
        return rcopy(ZTS, ZTR.at[j], zts.at[j], ztr.at[j], dev_z((z + step_of(j, nz)) % nz))

    def home(half, k):
        src, dst = ((OUT0, XR0), (OUT1, XR1))[half]
        return rcopy(src.at[(x + k) % nx], dst.at[k], xbs.at[half, k], xbr.at[half, k], dev_x(k))

    def combine(half):
        for j in range(1, nz):
            back(half, j).wait_recv()
        rows = ZRET[half].reshape(half_slots, width)
        return dot_nn(SWT[half], rows).astype(BF16).reshape(nx, TOK, width)

    def body(t, carry):
        @pl.when(t == min(2, per_half))
        def _():
            choose(1)

        @pl.when(t < nz)
        def _():
            half, r = t // per_half, t % per_half

            @pl.when(r > 0)
            def _():
                slot_rows(half, 2 * r).wait_recv()

            slot_rows(half, 2 * r + 1).wait_recv()

            @pl.when(q < TP - 1)
            def _():
                spread(q, t, 0).start()

            @pl.when(q > 0)
            def _():
                spread(q, t, 1).start()

        for k in range(1, TP):
            i = t - k

            @pl.when(jnp.logical_and(i >= 0, i < nz))
            def _():
                @pl.when(q >= k)
                def _():
                    spread(q - k, i, 0).wait_recv()

                    @pl.when(q < TP - 1)
                    def _():
                        spread(q - k, i, 0).start()

                @pl.when(q + k < TP)
                def _():
                    spread(q + k, i, 1).wait_recv()

                    @pl.when(q > 0)
                    def _():
                        spread(q + k, i, 1).start()

        i = t - (TP - 1)

        @pl.when(jnp.logical_and(i >= 0, i < nz))
        def _():
            @pl.when(i == 0)
            def _():
                for n in range(2, 5):
                    local[n].wait()
                    siblings[n].wait_recv()

            adjoint = dot_nt(RH[0, i].reshape(2 * sp, width), WD[:, pl.ds(0, width)])
            for s in range(1, TP):
                adjoint += dot_nt(RH[s, i].reshape(2 * sp, width), WD[:, pl.ds(s * width, width)])
            d_gate = (adjoint * A1[i]).astype(BF16)
            d_up = (adjoint * A2[i]).astype(BF16)
            RT[i] = jnp.broadcast_to(jnp.sum(adjoint * A3[i], axis=1, keepdims=True), (2 * sp, META))
            for s in range(TP):
                part = pl.ds(s * width, width)
                TM[s, i] = dot_nt(d_gate, WG[part, :]) + dot_nt(d_up, WU[part, :])

        @pl.when(t == nz + TP - 2)
        def _():
            RTS[...] = jnp.transpose(RT[...].reshape(nslot, META))[0:8, :]
            for k in range(1, TP):
                route_tp(k).start()

        for k in range(TP - 1):
            i = t - (TP - 1) - k

            @pl.when(jnp.logical_and(i >= 0, i < nz))
            def _():
                for way in range(2):
                    place = k if way == 0 else TP - 1 - k
                    src, dst = ((SR, RR), (SL, RL))[way]
                    targets = range(TP - 1, k, -1) if way == 0 else range(0, TP - 1 - k)

                    @pl.when(q == place)
                    def _():
                        for s in targets:
                            value = TM[s, i]
                            if k > 0:
                                passed(s, i, way).wait_recv()
                                value = value + dst[s, i].astype(F32)
                            src[s, i] = value.astype(BF16)
                            passed(s, i, way).start()

        i = t - 2 * (TP - 1)

        @pl.when(jnp.logical_and(i >= 0, i < nz))
        def _():
            @pl.when(q > 0)
            def _():
                passed(q, i, 0).wait_recv()
                TM[q, i] = TM[q, i] + RR[q, i].astype(F32)

            @pl.when(q < TP - 1)
            def _():
                passed(q, i, 1).wait_recv()
                TM[q, i] = TM[q, i] + RL[q, i].astype(F32)

            half, r = i // per_half, i % per_half
            ZS[i] = TM[q, i].astype(BF16).reshape(2, sp, width)
            back(half, 2 * r + 1).start()

            @pl.when(r == 0)
            def _():
                ZRET[half, 0] = ZS[i, 0]

            @pl.when(r > 0)
            def _():
                back(half, 2 * r).start()

        @pl.when(t == per_half + 2 * (TP - 1))
        def _():
            OUT0[...] = combine(0)
            for k in range(1, nx):
                home(0, k).start()

        @pl.when(t == nz + TP)
        def _():
            for k in range(1, TP):
                route_tp(k).wait_recv()
            ZTS[...] = RTS[...] + RTR[0] + RTR[1] + RTR[2]
            ZTR[0] = ZTS[...]
            for j in range(1, nz):
                route_z(j).start()

        return carry

    lax.fori_loop(0, nz + 2 * (TP - 1), body, 0)

    for j in range(1, nz):
        route_z(j).wait_recv()
    columns = jnp.transpose(ZTR[...].reshape(nz * 8, nslot))
    for half in range(2):
        ids_now = IDW[half, 0:8, :]
        route = jnp.zeros((8, ntok), F32)
        for j in range(nz):
            start = half * half_slots + j * sp
            column = columns[start:start + sp, 8 * j:8 * j + 1]
            value = jnp.sum(SMAT[half, j] * column, axis=0, keepdims=True)
            route += (ids_now == expert_at(j)).astype(F32) * value
        route_t = jnp.transpose(jnp.concatenate([route, jnp.zeros((META - 8, ntok), F32)], axis=0))
        lanes = pl.ds(width + META * (1 - half), META)
        OUT1[:, :, lanes] = route_t.astype(BF16).reshape(nx, TOK, META)
    OUT1[:, :, pl.ds(0, width)] = combine(1)
    for k in range(1, nx):
        home(1, k).start()
    near = OUT0[x].astype(F32)
    for k in range(1, nx):
        home(0, k).wait_recv()
        near += XR0[k].astype(F32)
    gin_ref[...] = near
    total = OUT1[x].astype(F32)
    for k in range(1, nx):
        home(1, k).wait_recv()
        total += XR1[k].astype(F32)
    HB[...] = total[:, 0:width + META].astype(BF16)
    homeward = rcopy(HB, HR, hs.at[1], hr.at[1], partner)
    homeward.start()
    homeward.wait_recv()
    gin_ref[...] += HR[:, pl.ds(0, width)].astype(F32)
    route_here = total[:, width + META:width + 2 * META] + HR[:, pl.ds(width, META)].astype(F32)
    grt_ref[...] = jnp.transpose(route_here)[0:8, :]

    to_partner.wait_send()
    homeward.wait_send()
    for copy in siblings:
        copy.wait_send()
    for k in range(1, TP):
        route_tp(k).wait_send()
    for half in range(2):
        for k in range(1, nx):
            along_x(half, k).wait_send()
            home(half, k).wait_send()
        for j in range(1, nz):
            slot_rows(half, j).wait_send()
            back(half, j).wait_send()
    for j in range(1, nz):
        route_z(j).wait_send()

    def drain(i, carry):
        for origin in range(TP):
            @pl.when(jnp.logical_and(q >= origin, q < TP - 1))
            def _():
                spread(origin, i, 0).wait_send()

            @pl.when(jnp.logical_and(q <= origin, q > 0))
            def _():
                spread(origin, i, 1).wait_send()

            @pl.when(q < origin)
            def _():
                passed(origin, i, 0).wait_send()

            @pl.when(q > origin)
            def _():
                passed(origin, i, 1).wait_send()

        return carry

    lax.fori_loop(0, nz, drain, 0)


def shards(grad_out, route_weights, expert_ids, w_gate, w_up, w_down, saved_gate, saved_up):
    width = grad_out.shape[1]
    nz = lax.axis_size("group") // 2
    nx = lax.axis_size("expert") // 2
    ntok, sp = nx * TOK, 2 * nx
    half_slots = nz * sp
    nslot = 2 * half_slots
    features = TP * width
    slots = saved_gate.shape[0]
    topk = expert_ids.shape[1]
    vmem = pltpu.VMEM
    dma = pltpu.SemaphoreType.DMA
    piece = (nz, 2, sp, width)
    flat = (nz, 2 * sp, width)
    wide = width + META
    scratch = [
        vmem((TOK, wide), BF16),
        vmem((topk, TOK), jnp.int32),
        vmem((topk, TOK), BF16),
        vmem((2, nx, TOK, wide), BF16),
        vmem((2, nz, sp, width), BF16),
        vmem((2, nz, sp, ntok), F32),
        vmem((2, ntok, half_slots), BF16),
        vmem((2, 16, ntok), F32),
        vmem((TP,) + piece, BF16),
        vmem((256, features), BF16),
        vmem((features, 256), BF16),
        vmem((features, 256), BF16),
        vmem((2, slots, 128), BF16),
        vmem((2, slots, 128), BF16),
        vmem((nz, 2 * sp, 256), F32),
        vmem((nz, 2 * sp, 256), F32),
        vmem((nz, 2 * sp, 256), F32),
        vmem((TP,) + flat, F32),
        vmem((nz, 2 * sp, META), F32),
        vmem((8, nslot), F32),
        vmem((TP - 1, 8, nslot), F32),
        vmem((8, nslot), F32),
        vmem((nz, 8, nslot), F32),
        vmem((TP,) + flat, BF16),
        vmem((TP,) + flat, BF16),
        vmem((TP,) + flat, BF16),
        vmem((TP,) + flat, BF16),
        vmem(piece, BF16),
        vmem((2, nz, sp, width), BF16),
        vmem((nx, TOK, width), BF16),
        vmem((nx, TOK, wide + META), BF16),
        vmem((nx, TOK, width), BF16),
        vmem((nx, TOK, wide + META), BF16),
        vmem((TOK, wide), BF16),
        vmem((TOK, wide), BF16),
        dma((8,)), dma((5,)), dma((5,)),
        dma((2,)), dma((2,)),
        dma((2, nx)), dma((2, nx)),
        dma((2, nz)), dma((2, nz)),
        dma((2, TP, nz)), dma((TP, nz)),
        dma((2, TP, nz)), dma((2, TP, nz)),
        dma((2, nz)), dma((2, nz)),
        dma((TP - 1,)), dma((TP - 1,)),
        dma((nz,)), dma((nz,)),
        dma((2, nx)), dma((2, nx)),
    ]
    whole = pl.BlockSpec(memory_space=pltpu.VMEM)
    far = pl.BlockSpec(memory_space=pltpu.HBM)
    grad_in, grad_route = pl.pallas_call(
        functools.partial(kernel, nx, nz, width),
        out_shape=(
            jax.ShapeDtypeStruct((TOK, width), F32),
            jax.ShapeDtypeStruct((topk, TOK), F32),
        ),
        in_specs=[far] * 8,
        out_specs=(whole, whole),
        scratch_shapes=scratch,
        compiler_params=pltpu.CompilerParams(
            collective_id=0, has_side_effects=True, vmem_limit_bytes=(64 * 1024 - 256) * 1024
        ),
        name="expert_backward",
    )(grad_out, expert_ids.T, route_weights.T, w_gate, w_up, w_down, saved_gate, saved_up)
    return grad_in, grad_route.T


def solution(mesh):
    return jax.shard_map(
        shards,
        mesh=mesh,
        in_specs=(
            P(("group", "expert"), "tp"),
            P(("group", "expert"), None),
            P(("group", "expert"), None),
            P(("group", "expert"), None, "tp"),
            P(("group", "expert"), None, "tp"),
            P(("group", "expert"), "tp", None),
            P(("group", "expert"), "tp"),
            P(("group", "expert"), "tp"),
        ),
        out_specs=(P(("group", "expert"), "tp"), P(("group", "expert"), None)),
        check_vma=False,
    )
```

```python
import functools

import jax
import jax.numpy as jnp
from jax import lax
from jax.experimental import pallas as pl
from jax.experimental.pallas import tpu as pltpu
from jax.sharding import PartitionSpec as P

MESH = pl.DeviceIdType.MESH
F32 = jnp.float32
BF16 = jnp.bfloat16
TP = 4
TOK = 16
META = 128


def dot_nn(left, right):
    return lax.dot_general(left, right, (((1,), (0,)), ((), ())), preferred_element_type=F32)


def dot_nt(left, right):
    return lax.dot_general(left, right, (((1,), (1,)), ((), ())), preferred_element_type=F32)


def dot_tn(left, right):
    return lax.dot_general(left, right, (((0,), (0,)), ((), ())), preferred_element_type=F32)


def rcopy(src, dst, send, recv, device):
    return pltpu.make_async_remote_copy(
        src_ref=src, dst_ref=dst, send_sem=send, recv_sem=recv, device_id=device, device_id_type=MESH
    )


def step_of(j, count):
    odd = j % 2
    return odd * ((j + 1) // 2) + (1 - odd) * ((count - j // 2) % count)


def kernel(
    nx, nz, width,
    go_hbm, ids_hbm, rw_hbm, wg_hbm, wu_hbm, wd_hbm, sg_hbm, su_hbm,
    gin_ref, grt_ref,
    tok, IDS, RW, T, SEL, SMAT, SWT, IDW, RH, WD, WG, WU, SG, SU, A1, A2, A3, TM, RT, RTS, RTR, ZTS, ZTR,
    SR, SL, RR, RL, ZS, ZRET, OUT0, OUT1, XR0, XR1, HB, HR,
    lsem, ws, wr, hs, hr, xs, xr, zs, zr, ags, agr, rss, rsr, zbs, zbr, rts, rtr, zts, ztr, xbs, xbr,
):
    g = lax.axis_index("group")
    e = lax.axis_index("expert")
    q = lax.axis_index("tp")
    h, z = g // nz, g % nz
    x, c = e // 2, e % 2
    ntok = nx * TOK
    sp = 2 * nx
    half_slots = nz * sp
    nslot = 2 * half_slots
    per_half = nz // 2
    lead = per_half // 2
    hid = 128
    slots = 2 * nslot

    def half_of(i):
        return ((i + lead) // per_half) % 2

    def pair_of(i):
        return (i + lead + lead * (1 - half_of(i))) % per_half

    def piece_of(half, j):
        return [i for i in range(nz) if half_of(i) == half and pair_of(i) == j // 2][0]

    def dev_x(k):
        return {"expert": ((x + k) % nx) * 2 + c}

    def dev_z(zz):
        return {"group": h * nz + zz}

    sibling = {"expert": x * 2 + (1 - c)}
    partner = {"group": (1 - h) * nz + z}

    pairs = (
        (sg_hbm, SG.at[0], SG.at[1]),
        (su_hbm, SU.at[0], SU.at[1]),
        (wd_hbm.at[0], WD.at[pl.ds(0, hid), :], WD.at[pl.ds(hid, hid), :]),
        (wg_hbm.at[0], WG.at[:, pl.ds(0, hid)], WG.at[:, pl.ds(hid, hid)]),
        (wu_hbm.at[0], WU.at[:, pl.ds(0, hid)], WU.at[:, pl.ds(hid, hid)]),
    )
    small = [
        pltpu.make_async_copy(go_hbm, tok.at[:, pl.ds(0, width)], lsem.at[5]),
        pltpu.make_async_copy(ids_hbm, IDS, lsem.at[6]),
        pltpu.make_async_copy(rw_hbm, RW, lsem.at[7]),
    ]
    for copy in small:
        copy.start()
    local = [pltpu.make_async_copy(src, own, lsem.at[i]) for i, (src, own, _) in enumerate(pairs)]
    for copy in local:
        copy.start()

    barrier = pltpu.get_barrier_semaphore()
    for k in range(1, nx):
        pl.semaphore_signal(barrier, inc=1, device_id=dev_x(k), device_id_type=MESH)
    for k in range(1, nz):
        pl.semaphore_signal(barrier, inc=1, device_id=dev_z((z + k) % nz), device_id_type=MESH)
    for k in range(1, TP):
        pl.semaphore_signal(barrier, inc=1, device_id={"tp": (q + k) % TP}, device_id_type=MESH)
    pl.semaphore_signal(barrier, inc=1, device_id=sibling, device_id_type=MESH)
    pl.semaphore_signal(barrier, inc=1, device_id=partner, device_id_type=MESH)
    for copy in small:
        copy.wait()
    lane = lax.broadcasted_iota(jnp.int32, (8, META), 1)
    entry = lax.broadcasted_iota(jnp.int32, (8, META), 0)
    tok[:, pl.ds(width, META)] = (
        dot_tn(IDS[...].astype(F32).astype(BF16), (lane == entry).astype(F32).astype(BF16))
        + dot_tn(RW[...], (lane == entry + 8).astype(F32).astype(BF16))
    ).astype(BF16)
    pl.semaphore_wait(barrier, nx + nz + TP - 1)

    def along_x(half, k):
        src = tok if half == 0 else T.at[1, x]
        return rcopy(src, T.at[half, x], xs.at[half, k], xr.at[half, x], dev_x(k))

    def arrives_x(half, k):
        origin = (x + k) % nx
        return rcopy(tok, T.at[half, origin], xs.at[half, k], xr.at[half, origin], dev_x(k))

    to_partner = rcopy(tok, T.at[1, x], hs.at[0], hr.at[0], partner)
    to_partner.start()
    for k in range(1, nx):
        along_x(0, k).start()
    T[0, x] = tok[...]
    siblings = [rcopy(src, far, ws.at[i], wr.at[i], sibling) for i, (src, _, far) in enumerate(pairs)]
    for copy in siblings:
        copy.start()
    to_partner.wait_recv()
    for k in range(1, nx):
        along_x(1, k).start()

    for i in range(2):
        local[i].wait()
        siblings[i].wait_recv()
    rest = lax.broadcasted_iota(jnp.int32, (sp, slots), 0)
    col = lax.broadcasted_iota(jnp.int32, (sp, slots), 1)
    within = ((rest >> 1) << 2) + (rest & 1) + c * 2
    pieces = []
    for i in range(nz):
        half = (h, 1 - h)[half_of(i)]
        for j in (2 * pair_of(i), 2 * pair_of(i) + 1):
            first = (half * nz + (z + step_of(j, nz)) % nz) * (4 * nx)
            pieces.append((within == col - first).astype(F32))
    pick = jnp.concatenate(pieces, axis=0).astype(BF16)
    for s in range(2):
        gate = dot_nn(pick, SG[s])
        up = dot_nn(pick, SU[s])
        sigma = jax.nn.sigmoid(gate)
        act = gate * sigma
        lanes = pl.ds(s * hid, hid)
        A1[:, :, lanes] = (up * sigma * (1.0 + gate * (1.0 - sigma))).reshape(nz, 2 * sp, hid)
        A2[:, :, lanes] = act.reshape(nz, 2 * sp, hid)
        A3[:, :, lanes] = (act * up).reshape(nz, 2 * sp, hid)

    def expert_at(j):
        zz = (z + nz - step_of(j, nz)) % nz
        return ((h * nz + zz) * nx + x).astype(F32)

    def slot_rows(half, j, i=None):
        i = piece_of(half, j) if i is None else i
        return rcopy(
            SEL.at[half, j], RH.at[q, i, j % 2], zs.at[half, j], zr.at[half, j],
            dev_z((z + nz - step_of(j, nz)) % nz),
        )

    def choose(half):
        for k in range(1, nx):
            arrives_x(half, k).wait_recv()
        meta_t = jnp.transpose(T[half, :, :, pl.ds(width, META)].reshape(ntok, META).astype(F32))
        IDW[half] = meta_t[0:16, :]
        ids8 = IDW[half, 0:8, :]
        w8 = IDW[half, 8:16, :]
        match_rows, weight_rows = [], []
        for j in range(nz):
            hit = (ids8 == expert_at(j)).astype(F32)
            match_rows.append(jnp.sum(hit, axis=0, keepdims=True))
            weight_rows.append(jnp.sum(hit * w8, axis=0, keepdims=True))
        t_row = lax.broadcasted_iota(jnp.int32, (ntok, ntok), 0)
        t_col = lax.broadcasted_iota(jnp.int32, (ntok, ntok), 1)
        before = jnp.logical_and(t_row >> 4 == t_col >> 4, t_row < t_col).astype(F32).astype(BF16)
        matches = jnp.concatenate(match_rows, axis=0)
        ranks = dot_nn(matches.astype(BF16), before)
        s_row = lax.broadcasted_iota(jnp.int32, (sp, ntok), 0)
        s_block = (s_row >> 1 == lax.broadcasted_iota(jnp.int32, (sp, ntok), 1) >> 4).astype(F32)
        s_level = (s_row & 1).astype(F32)
        for j in range(nz):
            SMAT[half, j] = s_block * matches[j:j + 1, :] * (s_level == ranks[j:j + 1, :]).astype(F32)
        tokens = T[half, :, :, pl.ds(0, width)].reshape(ntok, width)
        selected = dot_nn(SMAT[half].reshape(half_slots, ntok).astype(BF16), tokens).astype(BF16)
        SEL[half] = selected.reshape(nz, sp, width)
        for j in range(1, nz):
            slot_rows(half, j).start()
        RH[q, piece_of(half, 0), 0] = SEL[half, 0]
        weighted = jnp.concatenate([SMAT[half, j] * weight_rows[j] for j in range(nz)], axis=0)
        SWT[half] = jnp.transpose(weighted).astype(BF16)

    choose(0)

    def spread(origin, i, way):
        return rcopy(
            RH.at[origin, i], RH.at[origin, i], ags.at[way, origin, i], agr.at[origin, i],
            {"tp": (q + 1 - 2 * way) % TP},
        )

    def passed(s, i, way):
        src, dst = ((SR, RR), (SL, RL))[way]
        return rcopy(
            src.at[s, i], dst.at[s, i], rss.at[way, s, i], rsr.at[way, s, i], {"tp": (q + 1 - 2 * way) % TP}
        )

    def back(half, j, i=None):
        i = piece_of(half, j) if i is None else i
        return rcopy(
            ZS.at[i, j % 2], ZRET.at[half, j], zbs.at[half, j], zbr.at[half, j],
            dev_z((z + step_of(j, nz)) % nz),
        )

    def route_tp(half, k):
        return rcopy(
            RTS.at[half], RTR.at[half, k - 1], rts.at[half, k - 1], rtr.at[half, k - 1], {"tp": (q + k) % TP}
        )

    def route_z(half, j):
        return rcopy(
            ZTS.at[half], ZTR.at[half, j], zts.at[half, j], ztr.at[half, j], dev_z((z + step_of(j, nz)) % nz)
        )

    def route_out(half):
        parts = [RT[piece_of(half, 2 * r)] for r in range(per_half)]
        RTS[half] = jnp.transpose(jnp.concatenate(parts, axis=0))[0:8, :]
        for k in range(1, TP):
            route_tp(half, k).start()

    def route_on(half):
        for k in range(1, TP):
            route_tp(half, k).wait_recv()
        ZTS[half] = RTS[half] + RTR[half, 0] + RTR[half, 1] + RTR[half, 2]
        ZTR[half, 0] = ZTS[half]
        for j in range(1, nz):
            route_z(half, j).start()

    def route_back(half):
        for j in range(1, nz):
            route_z(half, j).wait_recv()
        columns = jnp.transpose(ZTR[half].reshape(nz * 8, half_slots))
        ids_now = IDW[half, 0:8, :]
        route = jnp.zeros((8, ntok), F32)
        for j in range(nz):
            column = columns[j * sp:(j + 1) * sp, 8 * j:8 * j + 1]
            value = jnp.sum(SMAT[half, j] * column, axis=0, keepdims=True)
            route += (ids_now == expert_at(j)).astype(F32) * value
        route_t = jnp.transpose(jnp.concatenate([route, jnp.zeros((META - 8, ntok), F32)], axis=0))
        return route_t.astype(BF16).reshape(nx, TOK, META)

    def home(half, k):
        src, dst = ((OUT0, XR0), (OUT1, XR1))[half]
        return rcopy(src.at[(x + k) % nx], dst.at[k], xbs.at[half, k], xbr.at[half, k], dev_x(k))

    def combine(half):
        for j in range(1, nz):
            back(half, j).wait_recv()
        rows = ZRET[half].reshape(half_slots, width)
        return dot_nn(SWT[half], rows).astype(BF16).reshape(nx, TOK, width)

    def body(t, carry):
        @pl.when(t == lead)
        def _():
            choose(1)

        @pl.when(t < nz)
        def _():
            half, r = half_of(t), pair_of(t)

            @pl.when(r > 0)
            def _():
                slot_rows(half, 2 * r, t).wait_recv()

            slot_rows(half, 2 * r + 1, t).wait_recv()

            @pl.when(q < TP - 1)
            def _():
                spread(q, t, 0).start()

            @pl.when(q > 0)
            def _():
                spread(q, t, 1).start()

        for k in range(1, TP):
            i = t - k

            @pl.when(jnp.logical_and(i >= 0, i < nz))
            def _():
                @pl.when(q >= k)
                def _():
                    spread(q - k, i, 0).wait_recv()

                    @pl.when(q < TP - 1)
                    def _():
                        spread(q - k, i, 0).start()

                @pl.when(q + k < TP)
                def _():
                    spread(q + k, i, 1).wait_recv()

                    @pl.when(q > 0)
                    def _():
                        spread(q + k, i, 1).start()

        i = t - (TP - 1)

        @pl.when(jnp.logical_and(i >= 0, i < nz))
        def _():
            @pl.when(i == 0)
            def _():
                for n in range(2, 5):
                    local[n].wait()
                    siblings[n].wait_recv()

            adjoint = dot_nt(RH[0, i].reshape(2 * sp, width), WD[:, pl.ds(0, width)])
            for s in range(1, TP):
                adjoint += dot_nt(RH[s, i].reshape(2 * sp, width), WD[:, pl.ds(s * width, width)])
            d_gate = (adjoint * A1[i]).astype(BF16)
            d_up = (adjoint * A2[i]).astype(BF16)
            RT[i] = jnp.broadcast_to(jnp.sum(adjoint * A3[i], axis=1, keepdims=True), (2 * sp, META))
            for s in range(TP):
                part = pl.ds(s * width, width)
                TM[s, i] = dot_nt(d_gate, WG[part, :]) + dot_nt(d_up, WU[part, :])

        @pl.when(t == nz + TP - 2)
        def _():
            route_out(0)

        @pl.when(t == lead + per_half + TP - 2)
        def _():
            route_out(1)

        for k in range(TP - 1):
            i = t - (TP - 1) - k

            @pl.when(jnp.logical_and(i >= 0, i < nz))
            def _():
                for way in range(2):
                    place = k if way == 0 else TP - 1 - k
                    src, dst = ((SR, RR), (SL, RL))[way]
                    targets = range(TP - 1, k, -1) if way == 0 else range(0, TP - 1 - k)

                    @pl.when(q == place)
                    def _():
                        for s in targets:
                            value = TM[s, i]
                            if k > 0:
                                passed(s, i, way).wait_recv()
                                value = value + dst[s, i].astype(F32)
                            src[s, i] = value.astype(BF16)
                            passed(s, i, way).start()

        i = t - 2 * (TP - 1)

        @pl.when(jnp.logical_and(i >= 0, i < nz))
        def _():
            @pl.when(q > 0)
            def _():
                passed(q, i, 0).wait_recv()
                TM[q, i] = TM[q, i] + RR[q, i].astype(F32)

            @pl.when(q < TP - 1)
            def _():
                passed(q, i, 1).wait_recv()
                TM[q, i] = TM[q, i] + RL[q, i].astype(F32)

            half, r = half_of(i), pair_of(i)
            ZS[i] = TM[q, i].astype(BF16).reshape(2, sp, width)
            back(half, 2 * r + 1, i).start()

            @pl.when(r == 0)
            def _():
                ZRET[half, 0] = ZS[i, 0]

            @pl.when(r > 0)
            def _():
                back(half, 2 * r, i).start()

        @pl.when(t == lead + per_half + TP)
        def _():
            route_on(1)

        @pl.when(t == nz + TP)
        def _():
            route_on(0)

        @pl.when(t == min(lead + per_half + 2 * (TP - 1), nz + 2 * (TP - 1) - 1))
        def _():
            OUT1[:, :, pl.ds(width, META)] = route_back(1)
            OUT1[:, :, pl.ds(0, width)] = combine(1)
            for k in range(1, nx):
                home(1, k).start()

        return carry

    lax.fori_loop(0, nz + 2 * (TP - 1), body, 0)

    OUT0[:, :, pl.ds(width, META)] = route_back(0)
    OUT0[:, :, pl.ds(0, width)] = combine(0)
    for k in range(1, nx):
        home(0, k).start()
    total = OUT1[x].astype(F32)
    for k in range(1, nx):
        home(1, k).wait_recv()
        total += XR1[k].astype(F32)
    HB[...] = total.astype(BF16)
    homeward = rcopy(HB, HR, hs.at[1], hr.at[1], partner)
    homeward.start()
    near = OUT0[x].astype(F32)
    for k in range(1, nx):
        home(0, k).wait_recv()
        near += XR0[k].astype(F32)
    homeward.wait_recv()
    near += HR[...].astype(F32)
    gin_ref[...] = near[:, 0:width]
    grt_ref[...] = jnp.transpose(near[:, width:width + META])[0:8, :]

    to_partner.wait_send()
    homeward.wait_send()
    for copy in siblings:
        copy.wait_send()
    for half in range(2):
        for k in range(1, TP):
            route_tp(half, k).wait_send()
        for k in range(1, nx):
            along_x(half, k).wait_send()
            home(half, k).wait_send()
        for j in range(1, nz):
            slot_rows(half, j).wait_send()
            back(half, j).wait_send()
            route_z(half, j).wait_send()

    def drain(i, carry):
        for origin in range(TP):
            @pl.when(jnp.logical_and(q >= origin, q < TP - 1))
            def _():
                spread(origin, i, 0).wait_send()

            @pl.when(jnp.logical_and(q <= origin, q > 0))
            def _():
                spread(origin, i, 1).wait_send()

            @pl.when(q < origin)
            def _():
                passed(origin, i, 0).wait_send()

            @pl.when(q > origin)
            def _():
                passed(origin, i, 1).wait_send()

        return carry

    lax.fori_loop(0, nz, drain, 0)


def shards(grad_out, route_weights, expert_ids, w_gate, w_up, w_down, saved_gate, saved_up):
    width = grad_out.shape[1]
    nz = lax.axis_size("group") // 2
    nx = lax.axis_size("expert") // 2
    ntok, sp = nx * TOK, 2 * nx
    half_slots = nz * sp
    nslot = 2 * half_slots
    features = TP * width
    slots = saved_gate.shape[0]
    topk = expert_ids.shape[1]
    vmem = pltpu.VMEM
    dma = pltpu.SemaphoreType.DMA
    piece = (nz, 2, sp, width)
    flat = (nz, 2 * sp, width)
    wide = width + META
    scratch = [
        vmem((TOK, wide), BF16),
        vmem((topk, TOK), jnp.int32),
        vmem((topk, TOK), BF16),
        vmem((2, nx, TOK, wide), BF16),
        vmem((2, nz, sp, width), BF16),
        vmem((2, nz, sp, ntok), F32),
        vmem((2, ntok, half_slots), BF16),
        vmem((2, 16, ntok), F32),
        vmem((TP,) + piece, BF16),
        vmem((256, features), BF16),
        vmem((features, 256), BF16),
        vmem((features, 256), BF16),
        vmem((2, slots, 128), BF16),
        vmem((2, slots, 128), BF16),
        vmem((nz, 2 * sp, 256), F32),
        vmem((nz, 2 * sp, 256), F32),
        vmem((nz, 2 * sp, 256), F32),
        vmem((TP,) + flat, F32),
        vmem((nz, 2 * sp, META), F32),
        vmem((2, 8, half_slots), F32),
        vmem((2, TP - 1, 8, half_slots), F32),
        vmem((2, 8, half_slots), F32),
        vmem((2, nz, 8, half_slots), F32),
        vmem((TP,) + flat, BF16),
        vmem((TP,) + flat, BF16),
        vmem((TP,) + flat, BF16),
        vmem((TP,) + flat, BF16),
        vmem(piece, BF16),
        vmem((2, nz, sp, width), BF16),
        vmem((nx, TOK, wide), BF16),
        vmem((nx, TOK, wide), BF16),
        vmem((nx, TOK, wide), BF16),
        vmem((nx, TOK, wide), BF16),
        vmem((TOK, wide), BF16),
        vmem((TOK, wide), BF16),
        dma((8,)), dma((5,)), dma((5,)),
        dma((2,)), dma((2,)),
        dma((2, nx)), dma((2, nx)),
        dma((2, nz)), dma((2, nz)),
        dma((2, TP, nz)), dma((TP, nz)),
        dma((2, TP, nz)), dma((2, TP, nz)),
        dma((2, nz)), dma((2, nz)),
        dma((2, TP - 1)), dma((2, TP - 1)),
        dma((2, nz)), dma((2, nz)),
        dma((2, nx)), dma((2, nx)),
    ]
    whole = pl.BlockSpec(memory_space=pltpu.VMEM)
    far = pl.BlockSpec(memory_space=pltpu.HBM)
    grad_in, grad_route = pl.pallas_call(
        functools.partial(kernel, nx, nz, width),
        out_shape=(
            jax.ShapeDtypeStruct((TOK, width), F32),
            jax.ShapeDtypeStruct((topk, TOK), F32),
        ),
        in_specs=[far] * 8,
        out_specs=(whole, whole),
        scratch_shapes=scratch,
        compiler_params=pltpu.CompilerParams(
            collective_id=0, has_side_effects=True, vmem_limit_bytes=(64 * 1024 - 256) * 1024
        ),
        name="expert_backward",
    )(grad_out, expert_ids.T, route_weights.T, w_gate, w_up, w_down, saved_gate, saved_up)
    return grad_in, grad_route.T


def solution(mesh):
    return jax.shard_map(
        shards,
        mesh=mesh,
        in_specs=(
            P(("group", "expert"), "tp"),
            P(("group", "expert"), None),
            P(("group", "expert"), None),
            P(("group", "expert"), None, "tp"),
            P(("group", "expert"), None, "tp"),
            P(("group", "expert"), "tp", None),
            P(("group", "expert"), "tp"),
            P(("group", "expert"), "tp"),
        ),
        out_specs=(P(("group", "expert"), "tp"), P(("group", "expert"), None)),
        check_vma=False,
    )
```
